32 devices in a mesh: parts: 2 (over x), group: 8 (over z, core), local: 2 (over y).
Axes of the slice: x: 2, y: 2, z: 4, core: 2. Of those that a mesh axis runs over, the one named last changes fastest.
Arguments:
- tokens: bfloat16 [128, 7168], P(('parts', 'group', 'local')), parts along dimension 0, may hold values from -6 to 6
- routes: int32 [128, 4], P(('parts', 'group', 'local')), parts along dimension 0, may hold values from 0 to 7, all different within a row; in each aligned block of 4 rows (0 to 3, 4 to 7, ...) at most 4 rows name the same one
- gate_weights: bfloat16 [128, 8], P(('parts', 'group', 'local')), parts along dimension 0, may hold values from 0.099609375 to 1
- w_gate: bfloat16 [16, 7168, 1024], P('group', None, 'local'), may hold values from -0.0625 to 0.0625
- w_up: bfloat16 [16, 7168, 1024], P('group', None, 'local'), may hold values from -0.0625 to 0.0625
- w_down: bfloat16 [16, 1024, 7168], P('group', 'local'), may hold values from -0.1875 to 0.1875
Outputs:
- mixed_rows: bfloat16 [128, 7168], P(('parts', 'group', 'local')), parts along dimension 0
The draws below stay inside these ranges and needn't reach their ends.
There are 2 independent parts, one for each index of `parts`. The reference program is written for one: setup_inputs(seed, part) draws one part's arguments, and reference() takes and returns one part's arrays. A program takes and returns all parts, laid end to end along the dimension named above; an argument that names none is the same for every part. Nothing has to cross between parts.
Inputs may be any that keep to these rules, and one draw needn't show every extreme that they name: `routes`: each row names 4 different groups; among the rows of one device no group is named by more than 4 rows, a bound that some block reaches.
All inputs are finite; a program needn't handle non-finite values.
Results may differ from the reference program's by a relative error of at most 0.005.
Values may be sent and summed in bfloat16 or wider, within the bound.
No kernel may reach another device: no remote copies, remote signals or barrier semaphores. Data moves between devices by JAX's collectives and lax.ppermute only.
A program may use at most 128 MiB of HBM per device.

```python
import math
import jax
import jax.numpy as jnp
import numpy as np
from jax import lax

D = 7168
HID = 1024
EXP_GROUP = 2
MAXG = 4
ROWS_DEV = 4
EXPERTS = 16
TOP = 8
CAP = 4
ROWS = 64
N_GROUP = 8


def block_levels(rng, dims, cuts, least, high):
    level = 1.0
    for dim, shards_of in cuts:
        steps = jax.random.uniform(jax.random.fold_in(jax.random.fold_in(rng, 6), dim), (shards_of,), jnp.float32, least / len(cuts), high / len(cuts))
        level = level * jnp.repeat(jnp.exp(steps), dims[dim] // shards_of).reshape((-1,) + (1,) * (len(dims) - 1 - dim))
    return level


def routed_block(rng, own, number, rows, count, top, bound, lean):
    ranking = jax.random.permutation(rng, count)
    heavy_load, common = load_shares(count, rows * top, bound, lean, True), load_shares(count, rows * top, bound, lean, False)
    places = jnp.arange(count)

    def named(lengths, offset_by):
        used = int((lengths > 0).sum())
        fixed = max(1, used // 4)
        shifted = fixed + (places - fixed + offset_by * (used - fixed)) % max(1, count - fixed)
        return jnp.zeros((count,), jnp.int32).at[ranking[jnp.where(places < fixed, places, shifted)]].set(jnp.asarray(lengths, jnp.int32))

    lengths = jnp.where(number % 4 == 0, named(heavy_load, number // 4), named(common, number - number // 4 - 1))
    mixed = jax.random.permutation(jax.random.fold_in(own, 3), count)
    donor, receiver = mixed[0:count // 2 * 2:2], mixed[1:count // 2 * 2:2]
    room = jnp.minimum(lengths[donor] - 1, bound - lengths[receiver]) // 2
    room = jnp.where((donor == ranking[0]) | (receiver == ranking[0]) | (lengths[receiver] == 0), 0, jnp.maximum(room, 0))
    shifted = jax.random.randint(jax.random.fold_in(own, 4), (count // 2,), 0, 1 << 20) % (room + 1)
    lengths = lengths.at[donor].add(-shifted).at[receiver].add(shifted)
    labels = jnp.searchsorted(jnp.cumsum(lengths), jnp.arange(rows * top), side="right").astype(jnp.int32)
    listing = labels.reshape(top, rows).T
    listing = listing[jax.random.permutation(jax.random.fold_in(own, 1), rows)]
    offset_by = jax.random.randint(jax.random.fold_in(own, 2), (rows, 1), 0, top)
    return jnp.take_along_axis(listing, (jnp.arange(top)[None, :] + offset_by) % top, axis=1)


def load_shares(count, total, limit, lean, full):
    portions = [(1 << 20) // math.isqrt(grade ** lean) + 1 for grade in range(1, count + 1)]
    largest = limit if full else min(limit, max(-(-total // count), total * portions[0] // sum(portions)))
    least = 1 if total - largest >= count - 1 else 0
    counts, surplus = [largest] + [least] * (count - 1), total - largest - least * (count - 1)
    while surplus > 0:
        candidates = [i for i in range(1, count) if counts[i] < largest] or [i for i in range(1, count) if counts[i] < limit]
        mass, left = sum([portions[i] for i in candidates]), surplus
        for i in candidates:
            extra = min(limit - counts[i], max(1, left * portions[i] // mass), surplus)
            counts[i] = counts[i] + extra
            surplus = surplus - extra
    return np.array(counts)


def normal_values(stream_key, extent, spread, bound, shards=(), kind=jnp.bfloat16):
    entries = spread * jax.random.normal(stream_key, extent, jnp.float32)
    if shards:
        entries = entries * block_levels(stream_key, extent, shards, -0.22, 0.18)
    return jnp.clip(entries, -bound, bound).astype(kind)


def setup_inputs(seed: int = 0, part: int = 0) -> dict:
    seeds = jax.random.split(jax.random.key(seed), 7)
    own_keys = jax.random.split(jax.random.fold_in(seeds[6], part), 7)
    tokens = normal_values(own_keys[0], (ROWS, D), 1.0, 6.0, ((0, 16),))
    routes_keys = jax.random.split(jax.random.fold_in(own_keys[1], 1), ROWS // ROWS_DEV)
    routes_turns = jax.random.permutation(jax.random.fold_in(own_keys[1], 3), ROWS // ROWS_DEV)
    routes = jax.vmap(lambda own, number: routed_block(jax.random.fold_in(own_keys[1], 2), own, number, ROWS_DEV, N_GROUP, MAXG, CAP, 2))(routes_keys, routes_turns).reshape((ROWS, MAXG))
    gate_weights = jnp.clip(jnp.exp(math.log(1.0) - 2.306499 * jax.random.uniform(own_keys[2], (ROWS, TOP), jnp.float32) ** block_levels(own_keys[2], (ROWS, TOP), ((0, 16),), -0.2, 0.2)), 0.099609375, 1.0).astype(jnp.bfloat16)
    w_gate = normal_values(seeds[3], (EXPERTS, D, HID), D ** -0.5, 0.0625, ((0, 8), (2, 2)))
    w_up = normal_values(seeds[4], (EXPERTS, D, HID), D ** -0.5, 0.0625, ((0, 8), (2, 2)))
    w_down = normal_values(seeds[5], (EXPERTS, HID, D), HID ** -0.5, 0.1875, ((0, 8), (1, 2)))
    return {"tokens": tokens, "routes": routes, "gate_weights": gate_weights, "w_gate": w_gate, "w_up": w_up, "w_down": w_down}


def reference(tokens, routes, gate_weights, w_gate, w_up, w_down):
    row_count = tokens.shape[0]
    model_width = tokens.shape[1]
    row_limit = min(row_count, (row_count // ROWS_DEV) * CAP)
    gate_pairs = gate_weights.astype(jnp.float32).reshape(row_count, MAXG, EXP_GROUP)

    def one_group(accumulated, group_index):
        member = routes == group_index
        pair_weights = jnp.sum(jnp.where(member[:, :, None], gate_pairs, jnp.float32(0.0)), axis=1)
        routed = jnp.any(member, axis=1).astype(jnp.int32)
        picked_rows = jnp.argsort(1 - routed, stable=True)[:row_limit].astype(jnp.int32)
        picked = tokens[picked_rows]
        picked_weights = pair_weights[picked_rows]
        contrib = jnp.zeros((row_limit, model_width), jnp.float32)
        for expert_slot in range(EXP_GROUP):
            expert_index = (group_index * EXP_GROUP + expert_slot).astype(jnp.int32)
            gate_matrix = lax.dynamic_index_in_dim(w_gate, expert_index, 0, keepdims=False)
            up_matrix = lax.dynamic_index_in_dim(w_up, expert_index, 0, keepdims=False)
            down_matrix = lax.dynamic_index_in_dim(w_down, expert_index, 0, keepdims=False)
            gate_act = jnp.dot(picked, gate_matrix, preferred_element_type=jnp.float32)
            up_act = jnp.dot(picked, up_matrix, preferred_element_type=jnp.float32)
            hidden = (jax.nn.silu(gate_act) * up_act).astype(jnp.bfloat16)
            expert_out = jnp.dot(hidden, down_matrix, preferred_element_type=jnp.float32)
            contrib = contrib + picked_weights[:, expert_slot:expert_slot + 1] * expert_out
        accumulated = accumulated.at[picked_rows].add(contrib)
        return accumulated, None

    start = jnp.zeros((row_count, model_width), jnp.float32)
    accumulated, _ = lax.scan(one_group, start, jnp.arange(N_GROUP, dtype=jnp.int32))
    return accumulated.astype(jnp.bfloat16)
```

```python
import jax
import jax.numpy as jnp
from jax import lax
from jax.experimental import pallas as pl
from jax.experimental.pallas import tpu as pltpu
from jax.sharding import PartitionSpec as P

LANES = 128


def rotate(value, axis, shift, stride):
    size = lax.axis_size(axis)
    return lax.ppermute(value, axis, [(i, (i + shift * stride) % size) for i in range(size)])


def other_core(value):
    return lax.ppermute(value, "group", [(i, i ^ 1) for i in range(lax.axis_size("group"))])


def experts_kernel(x_ref, gate_ref, up_ref, down_ref, keep_ref, send_ref):
    rows = x_ref.shape[0]
    width = down_ref.shape[1]
    pairs, _, hidden_here = gate_ref.shape
    keep_rows = keep_ref.shape[0]
    group = lax.axis_index("group").astype(jnp.float32)
    side = x_ref[:, width:].astype(jnp.float32)
    lane = lax.broadcasted_iota(jnp.int32, (rows, LANES), 1)
    groups_row = 4
    parts = []
    x = x_ref[:, :width]
    for e in range(pairs):
        weight = jnp.zeros((rows, 1), jnp.float32)
        for k in range(groups_row):
            hit = side[:, k : k + 1] == group
            column = groups_row + k * pairs + e
            weight = weight + jnp.where(hit, side[:, column : column + 1], 0.0)
        gate_act = jnp.dot(x, gate_ref[e], preferred_element_type=jnp.float32)
        up_act = jnp.dot(x, up_ref[e], preferred_element_type=jnp.float32)
        hidden = gate_act / (1.0 + jnp.exp(-gate_act)) * up_act
        parts.append((hidden * weight).astype(jnp.bfloat16))
    hidden = jnp.concatenate(parts, axis=1)
    step = 1024
    for c in range(0, width, step):
        y = jnp.dot(hidden, down_ref[:, c : c + step], preferred_element_type=jnp.float32)
        keep_ref[:, c : c + step] = y[:keep_rows]
        send_ref[:, c : c + step] = y[keep_rows:].astype(jnp.bfloat16)


def on_device(tokens, routes, gate_weights, w_gate, w_up, w_down):
    chips = lax.axis_size("group") // 2
    locals_ = lax.axis_size("local")
    rows_here, width = tokens.shape
    pairs, _, hidden_here = w_gate.shape
    side = routes.shape[1] + gate_weights.shape[1]
    mine = jnp.concatenate(
        [tokens, routes.astype(jnp.bfloat16), gate_weights, jnp.zeros((rows_here, LANES - side), jnp.bfloat16)], axis=1
    )
    line = jnp.concatenate([mine] + [rotate(mine, "group", k, 2) for k in range(1, chips)], axis=0)
    plane = jnp.concatenate([line] + [rotate(line, "local", k, 1) for k in range(1, locals_)], axis=0)
    x = jnp.concatenate([plane, other_core(plane)], axis=0)
    half = plane.shape[0]
    keep, send = pl.pallas_call(
        experts_kernel,
        out_shape=(
            jax.ShapeDtypeStruct((half, width), jnp.float32),
            jax.ShapeDtypeStruct((half, width), jnp.bfloat16),
        ),
        compiler_params=pltpu.CompilerParams(vmem_limit_bytes=6 << 20),
    )(x, w_gate, w_up, w_down.reshape(pairs * hidden_here, width))
    total = keep + other_core(send).astype(jnp.float32)
    blocks = total.reshape(locals_, chips * rows_here, width)
    total = blocks[0]
    for k in range(1, locals_):
        back = rotate(blocks[k].astype(jnp.bfloat16), "local", -k, 1)
        total = total + back.astype(jnp.float32)
    blocks = total.reshape(chips, rows_here, width)
    total = blocks[0]
    for k in range(1, chips):
        back = rotate(blocks[k].astype(jnp.bfloat16), "group", -k, 2)
        total = total + back.astype(jnp.float32)
    return total.astype(jnp.bfloat16)


def solution(mesh):
    return jax.shard_map(
        on_device,
        mesh=mesh,
        in_specs=(
            P(("parts", "group", "local"), None),
            P(("parts", "group", "local"), None),
            P(("parts", "group", "local"), None),
            P("group", None, "local"),
            P("group", None, "local"),
            P("group", "local", None),
        ),
        out_specs=P(("parts", "group", "local"), None),
        check_vma=False,
    )
```

```python
import functools

import jax
import jax.numpy as jnp
from jax import lax
from jax.experimental import pallas as pl
from jax.experimental.pallas import tpu as pltpu
from jax.sharding import PartitionSpec as P

LANES = 128
GROUPS_ROW = 4


def rotate(value, axis, shift, stride):
    size = lax.axis_size(axis)
    return lax.ppermute(value, axis, [(i, (i + shift * stride) % size) for i in range(size)])


def other_core(value):
    return lax.ppermute(value, "group", [(i, i ^ 1) for i in range(lax.axis_size("group"))])


def pack_kernel(tokens_ref, routes_ref, weights_ref, out_ref):
    rows, width = tokens_ref.shape
    side = routes_ref.shape[1] + weights_ref.shape[1]
    out_ref[:, :width] = tokens_ref[...]
    out_ref[:, width:] = jnp.concatenate(
        [
            routes_ref[...].astype(jnp.float32),
            weights_ref[...].astype(jnp.float32),
            jnp.zeros((rows, LANES - side), jnp.float32),
        ],
        axis=1,
    ).astype(jnp.bfloat16)


def pack(tokens, routes, gate_weights):
    rows, width = tokens.shape
    return pl.pallas_call(
        pack_kernel,
        out_shape=jax.ShapeDtypeStruct((rows, width + LANES), jnp.bfloat16),
        compiler_params=pltpu.CompilerParams(vmem_limit_bytes=2 << 20),
    )(tokens, routes, gate_weights)


def fetch_kernel(source_ref, after_ref, out_ref, sem):
    copy = pltpu.make_async_copy(source_ref, out_ref, sem)
    copy.start()
    copy.wait()


def fetch(weights, after, limit):
    nbytes = weights.size * 2
    return pl.pallas_call(
        fetch_kernel,
        out_shape=jax.ShapeDtypeStruct(weights.shape, weights.dtype),
        in_specs=[pl.BlockSpec(memory_space=pl.ANY)] * 2,
        out_specs=pl.BlockSpec(memory_space=pltpu.VMEM),
        scratch_shapes=[pltpu.SemaphoreType.DMA],
        compiler_params=pltpu.CompilerParams(vmem_limit_bytes=limit << 20),
        cost_estimate=pl.CostEstimate(flops=0, bytes_accessed=nbytes, transcendentals=0),
    )(weights, after)


def experts_kernel(count, *refs):
    pieces, (gate_ref, up_ref, down_hbm, keep_ref, send_ref, down_ref, x_ref, acts_ref, sems) = refs[:count], refs[count:]
    depth, width = down_ref.shape
    pairs = gate_ref.shape[0]
    hidden_here = depth // pairs
    keep_rows = keep_ref.shape[0]
    chunks = sems.shape[0]
    step = width // chunks

    def piece(c):
        columns = pl.ds(pl.multiple_of(c * step, LANES), step)
        return columns, pltpu.make_async_copy(down_hbm.at[:, columns], down_ref.at[:, columns], sems.at[c])

    for c in range(chunks):
        piece(c)[1].start()
    group = lax.axis_index("group").astype(jnp.float32)
    first = 0
    for part in pieces:
        x_ref[first : first + part.shape[0], :] = part[:, :width]
        first += part.shape[0]
    side = jnp.concatenate([part[:, width:] for part in pieces], axis=0).astype(jnp.float32)
    rows = x_ref.shape[0]
    acts_ref[...] = jnp.zeros_like(acts_ref)

    def enter(c, carry):
        depths = pl.ds(pl.multiple_of(c * step, LANES), step)
        x = x_ref[:, depths]
        for e in range(pairs):
            acts_ref[e, 0] += jnp.dot(x, gate_ref[e, depths, :], preferred_element_type=jnp.float32)
            acts_ref[e, 1] += jnp.dot(x, up_ref[e, depths, :], preferred_element_type=jnp.float32)
        return carry

    lax.fori_loop(0, chunks, enter, 0)
    hidden, weight = [], []
    for e in range(pairs):
        total = jnp.zeros((rows, 1), jnp.float32)
        for k in range(GROUPS_ROW):
            column = GROUPS_ROW + k * pairs + e
            total = total + jnp.where(side[:, k : k + 1] == group, side[:, column : column + 1], 0.0)
        weight.append(total)
        gate_act = acts_ref[e, 0]
        hidden.append((gate_act / (1.0 + jnp.exp(-gate_act)) * acts_ref[e, 1]).astype(jnp.bfloat16))

    def down(c, carry):
        columns, copy = piece(c)
        copy.wait()
        y = jnp.zeros((rows, step), jnp.float32)
        for e in range(pairs):
            part = down_ref[e * hidden_here : (e + 1) * hidden_here, columns]
            y = y + weight[e] * jnp.dot(hidden[e], part, preferred_element_type=jnp.float32)
        keep_ref[:, columns] = y[:keep_rows]
        send_ref[:, columns] = y[keep_rows:].astype(jnp.bfloat16)
        return carry

    lax.fori_loop(0, chunks, down, 0)


def on_device(tokens, routes, gate_weights, w_gate, w_up, w_down):
    chips = lax.axis_size("group") // 2
    locals_ = lax.axis_size("local")
    rows_here, width = tokens.shape
    pairs, _, hidden_here = w_gate.shape
    mine = pack(tokens, routes, gate_weights)
    others = [rotate(mine, "group", k, 2) for k in range(1, chips)]
    gate_here, others = lax.optimization_barrier((fetch(w_gate, mine, 34), others))
    line = jnp.concatenate([mine] + others, axis=0)
    crossed = [rotate(line, "local", k, 1) for k in range(1, locals_)]
    across_line = other_core(line)
    up_here, crossed = lax.optimization_barrier((fetch(w_up, line, 18), crossed))
    pieces = [line] + crossed + [across_line] + [other_core(part) for part in crossed]
    half = locals_ * chips * rows_here
    keep, send = pl.pallas_call(
        functools.partial(experts_kernel, len(pieces)),
        out_shape=(
            jax.ShapeDtypeStruct((half, width), jnp.float32),
            jax.ShapeDtypeStruct((half, width), jnp.bfloat16),
        ),
        in_specs=[pl.BlockSpec(memory_space=pltpu.VMEM)] * (len(pieces) + 2) + [pl.BlockSpec(memory_space=pl.ANY)],
        scratch_shapes=[
            pltpu.VMEM((pairs * hidden_here, width), jnp.bfloat16),
            pltpu.VMEM((2 * half, width), jnp.bfloat16),
            pltpu.VMEM((pairs, 2, 2 * half, hidden_here), jnp.float32),
            pltpu.SemaphoreType.DMA((7,)),
        ],
        compiler_params=pltpu.CompilerParams(vmem_limit_bytes=18 << 20),
    )(*pieces, gate_here, up_here, w_down.reshape(pairs * hidden_here, width))
    total = keep + other_core(send).astype(jnp.float32)
    blocks = total.reshape(locals_, chips * rows_here, width)
    total = blocks[0]
    for k in range(1, locals_):
        back = rotate(blocks[k].astype(jnp.bfloat16), "local", -k, 1)
        total = total + back.astype(jnp.float32)
    blocks = total.reshape(chips, rows_here, width)
    total = blocks[0]
    for k in range(1, chips):
        back = rotate(blocks[k].astype(jnp.bfloat16), "group", -k, 2)
        total = total + back.astype(jnp.float32)
    return total.astype(jnp.bfloat16)


def solution(mesh):
    return jax.shard_map(
        on_device,
        mesh=mesh,
        in_specs=(
            P(("parts", "group", "local"), None),
            P(("parts", "group", "local"), None),
            P(("parts", "group", "local"), None),
            P("group", None, "local"),
            P("group", None, "local"),
            P("group", "local", None),
        ),
        out_specs=P(("parts", "group", "local"), None),
        check_vma=False,
    )
```

```python
import functools

import jax
import jax.numpy as jnp
from jax import lax
from jax.experimental import pallas as pl
from jax.experimental.pallas import tpu as pltpu
from jax.sharding import PartitionSpec as P

LANES = 128
LEAST_ROWS = 128
GROUPS_ROW = 4


def rotate(value, axis, shift, stride):
    size = lax.axis_size(axis)
    return lax.ppermute(value, axis, [(i, (i + shift * stride) % size) for i in range(size)])


def other_core(value):
    return lax.ppermute(value, "group", [(i, i ^ 1) for i in range(lax.axis_size("group"))])


def pack(tokens, routes, gate_weights):
    zero = jnp.zeros((), jnp.bfloat16)
    width = tokens.shape[1]
    packed = lax.pad(tokens, zero, ((0, 0, 0), (0, LANES, 0)))
    first = width
    for side in (routes, gate_weights):
        last = first + side.shape[1]
        side = lax.pad(side, jnp.zeros((), side.dtype), ((0, 0, 0), (first, width + LANES - last, 0)))
        packed = packed + side.astype(jnp.bfloat16)
        first = last
    return packed


def fetch_kernel(source_ref, after_ref, out_ref, sem):
    copy = pltpu.make_async_copy(source_ref, out_ref, sem)
    copy.start()
    copy.wait()


def fetch(weights, after, limit):
    nbytes = weights.size * 2
    return pl.pallas_call(
        fetch_kernel,
        out_shape=jax.ShapeDtypeStruct(weights.shape, weights.dtype),
        in_specs=[pl.BlockSpec(memory_space=pl.ANY)] * 2,
        out_specs=pl.BlockSpec(memory_space=pltpu.VMEM),
        scratch_shapes=[pltpu.SemaphoreType.DMA],
        compiler_params=pltpu.CompilerParams(vmem_limit_bytes=limit << 20),
        cost_estimate=pl.CostEstimate(flops=0, bytes_accessed=nbytes, transcendentals=0),
    )(weights, after)


def experts_kernel(count, *refs):
    pieces, (gate_ref, up_ref, down_hbm), outs = refs[:count], refs[count : count + 3], refs[count + 3 : -4]
    down_ref, x_ref, acts_ref, sems = refs[-4:]
    depth, width = down_ref.shape
    pairs = gate_ref.shape[0]
    hidden_here = depth // pairs
    block = outs[0].shape[0]
    chunks = sems.shape[0]
    step = width // chunks

    def piece(c):
        columns = pl.ds(pl.multiple_of(c * step, LANES), step)
        return columns, pltpu.make_async_copy(down_hbm.at[:, columns], down_ref.at[:, columns], sems.at[c])

    for c in range(chunks):
        piece(c)[1].start()
    group = lax.axis_index("group").astype(jnp.float32)
    first = 0
    while first < x_ref.shape[0]:
        for part in pieces:
            x_ref[first : first + part.shape[0], :] = part[:, :width]
            first += part.shape[0]
    side = jnp.concatenate([part[:, width:] for part in pieces], axis=0).astype(jnp.float32)
    rows = side.shape[0]
    acts_ref[...] = jnp.zeros_like(acts_ref)

    half = width // 2

    def enter(c, carry):
        depths = pl.ds(pl.multiple_of(c * half, LANES), half)
        x = x_ref[:, depths]
        for e in range(pairs):
            acts_ref[e, 0] += jnp.dot(x, gate_ref[e, depths, :], preferred_element_type=jnp.float32)
            acts_ref[e, 1] += jnp.dot(x, up_ref[e, depths, :], preferred_element_type=jnp.float32)
        return carry

    lax.fori_loop(0, 2, enter, 0)
    hidden, weight = [], []
    for e in range(pairs):
        total = jnp.zeros((rows, 1), jnp.float32)
        for k in range(GROUPS_ROW):
            column = GROUPS_ROW + k * pairs + e
            total = total + jnp.where(side[:, k : k + 1] == group, side[:, column : column + 1], 0.0)
        weight.append(total)
        gate_act = acts_ref[e, 0]
        hidden.append((gate_act / (1.0 + jnp.exp(-gate_act)) * acts_ref[e, 1]).astype(jnp.bfloat16))

    def down(c, carry):
        columns, copy = piece(c)
        copy.wait()
        y = jnp.zeros((rows, step), jnp.float32)
        for e in range(pairs):
            part = down_ref[e * hidden_here : (e + 1) * hidden_here, columns]
            y = y + weight[e] * jnp.dot(hidden[e], part, preferred_element_type=jnp.float32)[:rows]
        for i, out in enumerate(outs):
            out[:, columns] = y[i * block : (i + 1) * block].astype(out.dtype)
        return carry

    lax.fori_loop(0, chunks, down, 0)


def join_kernel(blocks, *refs):
    total = refs[0][...]
    for ref in refs[1:-blocks]:
        total = total + ref[...].astype(jnp.float32)
    height = total.shape[0] // blocks
    for i, out in enumerate(refs[-blocks:]):
        out[...] = total[i * height : (i + 1) * height].astype(out.dtype)


def join(values, blocks, first):
    shape = (values[0].shape[0] // blocks, values[0].shape[1])
    return pl.pallas_call(
        functools.partial(join_kernel, blocks),
        out_shape=[
            jax.ShapeDtypeStruct(shape, jnp.bfloat16 if first + i else jnp.float32) for i in range(blocks)
        ],
        compiler_params=pltpu.CompilerParams(vmem_limit_bytes=4 << 20),
    )(*values)


def on_device(tokens, routes, gate_weights, w_gate, w_up, w_down):
    chips = lax.axis_size("group") // 2
    locals_ = lax.axis_size("local")
    rows_here, width = tokens.shape
    pairs, _, hidden_here = w_gate.shape
    mine = pack(tokens, routes, gate_weights)
    others = [rotate(mine, "group", k, 2) for k in range(1, chips)]
    gate_here, others = lax.optimization_barrier((fetch(w_gate, mine, 34), others))
    line = jnp.concatenate([mine] + others, axis=0)
    crossed = [rotate(line, "local", k, 1) for k in range(1, locals_)]
    across_line = other_core(line)
    up_here, crossed = lax.optimization_barrier((fetch(w_up, line, 26), crossed))
    pieces = [line] + crossed + [across_line] + [other_core(part) for part in crossed]
    block = chips * rows_here
    rows = 2 * locals_ * block
    padded = rows * max(1, LEAST_ROWS // rows)
    outs = pl.pallas_call(
        functools.partial(experts_kernel, len(pieces)),
        out_shape=[jax.ShapeDtypeStruct((block, width), jnp.float32)] * locals_
        + [jax.ShapeDtypeStruct((block, width), jnp.bfloat16)] * locals_,
        in_specs=[pl.BlockSpec(memory_space=pltpu.VMEM)] * (len(pieces) + 2) + [pl.BlockSpec(memory_space=pl.ANY)],
        scratch_shapes=[
            pltpu.VMEM((pairs * hidden_here, width), jnp.bfloat16),
            pltpu.VMEM((padded, width), jnp.bfloat16),
            pltpu.VMEM((pairs, 2, padded, hidden_here), jnp.float32),
            pltpu.SemaphoreType.DMA((7,)),
        ],
        compiler_params=pltpu.CompilerParams(vmem_limit_bytes=18 << 20),
    )(*pieces, gate_here, up_here, w_down.reshape(pairs * hidden_here, width))
    totals = [None] * locals_
    for k in reversed(range(locals_)):
        totals[k] = outs[k] + other_core(outs[locals_ + k]).astype(jnp.float32)
    home = [None] * chips
    backs = None
    for low, high in ((chips // 2, chips), (0, chips // 2)):
        if low == high:
            continue
        part = slice(low * rows_here, high * rows_here)
        sent = [totals[k][part].astype(jnp.bfloat16) for k in range(1, locals_)]
        if backs is not None:
            sent, backs = lax.optimization_barrier((sent, backs))
        backs = [rotate(sent[k - 1], "local", -k, 1) for k in range(1, locals_)]
        home[low:high] = join([totals[0][part]] + backs, high - low, low)
    result = home[0]
    for c in range(1, chips):
        result = result + rotate(home[c], "group", -c, 2).astype(jnp.float32)
    return result.astype(jnp.bfloat16)


def solution(mesh):
    return jax.shard_map(
        on_device,
        mesh=mesh,
        in_specs=(
            P(("parts", "group", "local"), None),
            P(("parts", "group", "local"), None),
            P(("parts", "group", "local"), None),
            P("group", None, "local"),
            P("group", None, "local"),
            P("group", "local", None),
        ),
        out_specs=P(("parts", "group", "local"), None),
        check_vma=False,
    )
```

```python
import functools

import jax
import jax.numpy as jnp
from jax import lax
from jax.experimental import pallas as pl
from jax.experimental.pallas import tpu as pltpu
from jax.sharding import PartitionSpec as P

LANES = 128
LEAST_ROWS = 128
GROUPS_ROW = 4


def rotate(value, axis, shift, stride):
    size = lax.axis_size(axis)
    return lax.ppermute(value, axis, [(i, (i + shift * stride) % size) for i in range(size)])


def chip_shift(value, k, back):
    size = lax.axis_size("group")
    chips = size // 2
    if chips & (chips - 1):
        return rotate(value, "group", -k if back else k, 2)
    return lax.ppermute(value, "group", [(i, i ^ (2 * k)) for i in range(size)])


def other_core(value):
    return lax.ppermute(value, "group", [(i, i ^ 1) for i in range(lax.axis_size("group"))])


def pack(tokens, routes, gate_weights):
    zero = jnp.zeros((), jnp.bfloat16)
    width = tokens.shape[1]
    column = lax.broadcasted_iota(jnp.int32, (tokens.shape[0], width + LANES), 1)
    inside = jnp.where(column < width, 0, 1)
    packed = lax.pad(tokens, zero, ((0, 0, 0), (0, LANES, 0)))
    first = width
    for side in (routes, gate_weights):
        last = first + side.shape[1]
        side = lax.pad(side, jnp.zeros((), side.dtype), ((0, 0, 0), (first, width + LANES - last, 0)))
        if side.dtype == jnp.int32:
            side = (side * inside).astype(jnp.bfloat16)
        packed = packed + side
        first = last
    return packed


def fetch_kernel(source_ref, after_ref, out_ref, sem):
    copy = pltpu.make_async_copy(source_ref, out_ref, sem)
    copy.start()
    copy.wait()


def fetch(weights, after, limit):
    nbytes = weights.size * 2
    return pl.pallas_call(
        fetch_kernel,
        out_shape=jax.ShapeDtypeStruct(weights.shape, weights.dtype),
        in_specs=[pl.BlockSpec(memory_space=pl.ANY)] * 2,
        out_specs=pl.BlockSpec(memory_space=pltpu.VMEM),
        scratch_shapes=[pltpu.SemaphoreType.DMA],
        compiler_params=pltpu.CompilerParams(vmem_limit_bytes=limit << 20),
        cost_estimate=pl.CostEstimate(flops=0, bytes_accessed=nbytes, transcendentals=0),
    )(weights, after)


def experts_kernel(count, *refs):
    pieces, (gate_ref, up_ref, down_hbm), outs = refs[:count], refs[count : count + 3], refs[count + 3 : -4]
    down_ref, x_ref, acts_ref, sems = refs[-4:]
    depth, width = down_ref.shape
    pairs = gate_ref.shape[0]
    hidden_here = depth // pairs
    block = outs[0].shape[0]
    chunks = sems.shape[0]
    step = width // chunks

    def piece(c):
        columns = pl.ds(pl.multiple_of(c * step, LANES), step)
        return columns, pltpu.make_async_copy(down_hbm.at[:, columns], down_ref.at[:, columns], sems.at[c])

    for c in range(chunks):
        piece(c)[1].start()
    group = lax.axis_index("group").astype(jnp.float32)
    first = 0
    while first < x_ref.shape[0]:
        for part in pieces:
            x_ref[first : first + part.shape[0], :] = part[:, :width]
            first += part.shape[0]
    side = jnp.concatenate([part[:, width:] for part in pieces], axis=0).astype(jnp.float32)
    rows = side.shape[0]
    acts_ref[...] = jnp.zeros_like(acts_ref)

    half = width // 2

    def enter(c, carry):
        depths = pl.ds(pl.multiple_of(c * half, LANES), half)
        x = x_ref[:, depths]
        for e in range(pairs):
            acts_ref[e, 0] += jnp.dot(x, gate_ref[e, depths, :], preferred_element_type=jnp.float32)
            acts_ref[e, 1] += jnp.dot(x, up_ref[e, depths, :], preferred_element_type=jnp.float32)
        return carry

    lax.fori_loop(0, 2, enter, 0)
    hidden, weight = [], []
    for e in range(pairs):
        total = jnp.zeros((rows, 1), jnp.float32)
        for k in range(GROUPS_ROW):
            column = GROUPS_ROW + k * pairs + e
            total = total + jnp.where(side[:, k : k + 1] == group, side[:, column : column + 1], 0.0)
        weight.append(total)
        gate_act = acts_ref[e, 0]
        hidden.append((gate_act / (1.0 + jnp.exp(-gate_act)) * acts_ref[e, 1]).astype(jnp.bfloat16))

    def down(c, carry):
        columns, copy = piece(c)
        copy.wait()
        y = jnp.zeros((rows, step), jnp.float32)
        for e in range(pairs):
            part = down_ref[e * hidden_here : (e + 1) * hidden_here, columns]
            y = y + weight[e] * jnp.dot(hidden[e], part, preferred_element_type=jnp.float32)[:rows]
        for i, out in enumerate(outs):
            out[:, columns] = y[i * block : (i + 1) * block].astype(out.dtype)
        return carry

    lax.fori_loop(0, chunks, down, 0)


def join_kernel(blocks, *refs):
    total = refs[0][...]
    for ref in refs[1:-blocks]:
        total = total + ref[...].astype(jnp.float32)
    height = total.shape[0] // blocks
    for i, out in enumerate(refs[-blocks:]):
        out[...] = total[i * height : (i + 1) * height].astype(out.dtype)


def join(values, blocks, first):
    shape = (values[0].shape[0] // blocks, values[0].shape[1])
    return pl.pallas_call(
        functools.partial(join_kernel, blocks),
        out_shape=[
            jax.ShapeDtypeStruct(shape, jnp.bfloat16 if first + i else jnp.float32) for i in range(blocks)
        ],
        compiler_params=pltpu.CompilerParams(vmem_limit_bytes=4 << 20),
    )(*values)


def on_device(tokens, routes, gate_weights, w_gate, w_up, w_down):
    chips = lax.axis_size("group") // 2
    locals_ = lax.axis_size("local")
    rows_here, width = tokens.shape
    pairs, _, hidden_here = w_gate.shape
    mine = pack(tokens, routes, gate_weights)
    others = [chip_shift(mine, k, False) for k in range(1, chips)]
    gate_here, others = lax.optimization_barrier((fetch(w_gate, mine, 34), others))
    line = jnp.concatenate([mine] + others, axis=0)
    crossed = [rotate(line, "local", k, 1) for k in range(1, locals_)]
    across_line = other_core(line)
    up_here, crossed = lax.optimization_barrier((fetch(w_up, line, 26), crossed))
    pieces = [line] + crossed + [across_line] + [other_core(part) for part in crossed]
    block = chips * rows_here
    rows = 2 * locals_ * block
    padded = rows * max(1, LEAST_ROWS // rows)
    outs = pl.pallas_call(
        functools.partial(experts_kernel, len(pieces)),
        out_shape=[jax.ShapeDtypeStruct((block, width), jnp.float32)] * locals_
        + [jax.ShapeDtypeStruct((block, width), jnp.bfloat16)] * locals_,
        in_specs=[pl.BlockSpec(memory_space=pltpu.VMEM)] * (len(pieces) + 2) + [pl.BlockSpec(memory_space=pl.ANY)],
        scratch_shapes=[
            pltpu.VMEM((pairs * hidden_here, width), jnp.bfloat16),
            pltpu.VMEM((padded, width), jnp.bfloat16),
            pltpu.VMEM((pairs, 2, padded, hidden_here), jnp.float32),
            pltpu.SemaphoreType.DMA((7,)),
        ],
        compiler_params=pltpu.CompilerParams(vmem_limit_bytes=18 << 20),
    )(*pieces, gate_here, up_here, w_down.reshape(pairs * hidden_here, width))
    totals = [None] * locals_
    for k in reversed(range(locals_)):
        totals[k] = outs[k] + other_core(outs[locals_ + k]).astype(jnp.float32)
    home = [None] * chips
    backs = None
    for low, high in ((chips // 2, chips), (0, chips // 2)):
        if low == high:
            continue
        part = slice(low * rows_here, high * rows_here)
        sent = [totals[k][part].astype(jnp.bfloat16) for k in range(1, locals_)]
        if backs is not None:
            sent, backs = lax.optimization_barrier((sent, backs))
        backs = [rotate(sent[k - 1], "local", -k, 1) for k in range(1, locals_)]
        home[low:high] = join([totals[0][part]] + backs, high - low, low)
    result = home[0]
    for c in range(1, chips):
        result = result + chip_shift(home[c], c, True).astype(jnp.float32)
    return result.astype(jnp.bfloat16)


def solution(mesh):
    return jax.shard_map(
        on_device,
        mesh=mesh,
        in_specs=(
            P(("parts", "group", "local"), None),
            P(("parts", "group", "local"), None),
            P(("parts", "group", "local"), None),
            P("group", None, "local"),
            P("group", None, "local"),
            P("group", "local", None),
        ),
        out_specs=P(("parts", "group", "local"), None),
        check_vma=False,
    )
```

```python
import functools

import jax
import jax.numpy as jnp
from jax import lax
from jax.experimental import pallas as pl
from jax.experimental.pallas import tpu as pltpu
from jax.sharding import PartitionSpec as P

LANES = 128
LEAST_ROWS = 128
GROUPS_ROW = 4


def rotate(value, axis, shift, stride):
    size = lax.axis_size(axis)
    return lax.ppermute(value, axis, [(i, (i + shift * stride) % size) for i in range(size)])


def chip_shift(value, k, back):
    size = lax.axis_size("group")
    chips = size // 2
    if chips & (chips - 1):
        return rotate(value, "group", -k if back else k, 2)
    return lax.ppermute(value, "group", [(i, i ^ (2 * k)) for i in range(size)])


def other_core(value):
    return lax.ppermute(value, "group", [(i, i ^ 1) for i in range(lax.axis_size("group"))])


def pack(tokens, routes, gate_weights):
    zero = jnp.zeros((), jnp.bfloat16)
    width = tokens.shape[1]
    column = lax.broadcasted_iota(jnp.int32, (tokens.shape[0], width + LANES), 1)
    inside = jnp.where(column < width, 0, 1)
    packed = lax.pad(tokens, zero, ((0, 0, 0), (0, LANES, 0)))
    first = width
    for side in (routes, gate_weights):
        last = first + side.shape[1]
        side = lax.pad(side, jnp.zeros((), side.dtype), ((0, 0, 0), (first, width + LANES - last, 0)))
        if side.dtype == jnp.int32:
            side = (side * inside).astype(jnp.bfloat16)
        packed = packed + side
        first = last
    return packed


def fetch_kernel(source_ref, after_ref, out_ref, sem):
    copy = pltpu.make_async_copy(source_ref, out_ref, sem)
    copy.start()
    copy.wait()


def fetch(weights, after, limit):
    nbytes = weights.size * 2
    return pl.pallas_call(
        fetch_kernel,
        out_shape=jax.ShapeDtypeStruct(weights.shape, weights.dtype),
        in_specs=[pl.BlockSpec(memory_space=pl.ANY)] * 2,
        out_specs=pl.BlockSpec(memory_space=pltpu.VMEM),
        scratch_shapes=[pltpu.SemaphoreType.DMA],
        compiler_params=pltpu.CompilerParams(vmem_limit_bytes=limit << 20),
        cost_estimate=pl.CostEstimate(flops=0, bytes_accessed=nbytes, transcendentals=0),
    )(weights, after)


def experts_kernel(count, *refs):
    pieces, (gate_ref, up_ref, down_hbm), outs = refs[:count], refs[count : count + 3], refs[count + 3 : -4]
    down_ref, x_ref, acts_ref, sems = refs[-4:]
    depth, width = down_ref.shape
    pairs = gate_ref.shape[0]
    hidden_here = depth // pairs
    block = outs[0].shape[0]
    chunks = sems.shape[0]
    step = width // chunks

    def piece(c):
        columns = pl.ds(pl.multiple_of(c * step, LANES), step)
        return columns, pltpu.make_async_copy(down_hbm.at[:, columns], down_ref.at[:, columns], sems.at[c])

    for c in range(chunks):
        piece(c)[1].start()
    group = lax.axis_index("group").astype(jnp.float32)
    first = 0
    while first < x_ref.shape[0]:
        for part in pieces:
            x_ref[first : first + part.shape[0], :] = part[:, :width]
            first += part.shape[0]
    side = jnp.concatenate([part[:, width:] for part in pieces], axis=0).astype(jnp.float32)
    rows = side.shape[0]
    acts_ref[...] = jnp.zeros_like(acts_ref)

    half = width // 2

    def enter(c, carry):
        depths = pl.ds(pl.multiple_of(c * half, LANES), half)
        x = x_ref[:, depths]
        for e in range(pairs):
            acts_ref[e, 0] += jnp.dot(x, gate_ref[e, depths, :], preferred_element_type=jnp.float32)
            acts_ref[e, 1] += jnp.dot(x, up_ref[e, depths, :], preferred_element_type=jnp.float32)
        return carry

    lax.fori_loop(0, 2, enter, 0)
    hidden, weight = [], []
    for e in range(pairs):
        total = jnp.zeros((rows, 1), jnp.float32)
        for k in range(GROUPS_ROW):
            column = GROUPS_ROW + k * pairs + e
            total = total + jnp.where(side[:, k : k + 1] == group, side[:, column : column + 1], 0.0)
        weight.append(total)
        gate_act = acts_ref[e, 0]
        hidden.append((gate_act / (1.0 + jnp.exp(-gate_act)) * acts_ref[e, 1]).astype(jnp.bfloat16))

    def down(c, carry):
        columns, copy = piece(c)
        copy.wait()
        y = jnp.zeros((rows, step), jnp.float32)
        for e in range(pairs):
            part = down_ref[e * hidden_here : (e + 1) * hidden_here, columns]
            y = y + weight[e] * jnp.dot(hidden[e], part, preferred_element_type=jnp.float32)[:rows]
        for i, out in enumerate(outs):
            out[:, columns] = y[i * block : (i + 1) * block].astype(out.dtype)
        return carry

    lax.fori_loop(0, chunks, down, 0)


def join_kernel(blocks, *refs):
    total = refs[0][...]
    for ref in refs[1:-blocks]:
        total = total + ref[...].astype(jnp.float32)
    height = total.shape[0] // blocks
    for i, out in enumerate(refs[-blocks:]):
        out[...] = total[i * height : (i + 1) * height].astype(out.dtype)


def join(values, blocks, first):
    shape = (values[0].shape[0] // blocks, values[0].shape[1])
    return pl.pallas_call(
        functools.partial(join_kernel, blocks),
        out_shape=[
            jax.ShapeDtypeStruct(shape, jnp.bfloat16 if first + i else jnp.float32) for i in range(blocks)
        ],
        compiler_params=pltpu.CompilerParams(vmem_limit_bytes=4 << 20),
    )(*values)


def on_device(tokens, routes, gate_weights, w_gate, w_up, w_down):
    chips = lax.axis_size("group") // 2
    locals_ = lax.axis_size("local")
    rows_here, width = tokens.shape
    pairs, _, hidden_here = w_gate.shape
    mine = pack(tokens, routes, gate_weights)
    others = [chip_shift(mine, k, False) for k in range(1, chips)]
    gate_here, others = lax.optimization_barrier((fetch(w_gate, mine, 34), others))
    line = jnp.concatenate([mine] + others, axis=0)
    crossed = [rotate(line, "local", k, 1) for k in range(1, locals_)]
    across_line = other_core(line)
    up_here, crossed = lax.optimization_barrier((fetch(w_up, line, 28), crossed))
    pieces = [line] + crossed + [across_line] + [other_core(part) for part in crossed]
    block = chips * rows_here
    rows = 2 * locals_ * block
    padded = rows * max(1, LEAST_ROWS // rows)
    outs = pl.pallas_call(
        functools.partial(experts_kernel, len(pieces)),
        out_shape=[jax.ShapeDtypeStruct((block, width), jnp.float32)] * locals_
        + [jax.ShapeDtypeStruct((block, width), jnp.bfloat16)] * locals_,
        in_specs=[pl.BlockSpec(memory_space=pltpu.VMEM)] * (len(pieces) + 2) + [pl.BlockSpec(memory_space=pl.ANY)],
        scratch_shapes=[
            pltpu.VMEM((pairs * hidden_here, width), jnp.bfloat16),
            pltpu.VMEM((padded, width), jnp.bfloat16),
            pltpu.VMEM((pairs, 2, padded, hidden_here), jnp.float32),
            pltpu.SemaphoreType.DMA((2 if padded <= LEAST_ROWS else 7,)),
        ],
        compiler_params=pltpu.CompilerParams(vmem_limit_bytes=19 << 20),
    )(*pieces, gate_here, up_here, w_down.reshape(pairs * hidden_here, width))
    totals = [None] * locals_
    for k in reversed(range(locals_)):
        totals[k] = outs[k] + other_core(outs[locals_ + k]).astype(jnp.float32)
    home = [None] * chips
    done = None
    for low, high in ((chips // 2, chips), (0, chips // 2)):
        if low == high:
            continue
        part = slice(low * rows_here, high * rows_here)
        sent = [totals[k][part].astype(jnp.bfloat16) for k in range(1, locals_)]
        if done is not None:
            sent, done = lax.optimization_barrier((sent, done))
        backs = [rotate(sent[k - 1], "local", -k, 1) for k in range(1, locals_)]
        home[low:high] = join([totals[0][part]] + backs, high - low, low)
        done = home[high - 1]
    result = home[0]
    for c in range(1, chips):
        result = result + chip_shift(home[c], c, True).astype(jnp.float32)
    return result.astype(jnp.bfloat16)


def solution(mesh):
    return jax.shard_map(
        on_device,
        mesh=mesh,
        in_specs=(
            P(("parts", "group", "local"), None),
            P(("parts", "group", "local"), None),
            P(("parts", "group", "local"), None),
            P("group", None, "local"),
            P("group", None, "local"),
            P("group", "local", None),
        ),
        out_specs=P(("parts", "group", "local"), None),
        check_vma=False,
    )
```

```python
import functools

import jax
import jax.numpy as jnp
from jax import lax
from jax.experimental import pallas as pl
from jax.experimental.pallas import tpu as pltpu
from jax.sharding import PartitionSpec as P

LANES = 128
LEAST_ROWS = 128
GROUPS_ROW = 4


def rotate(value, axis, shift, stride):
    size = lax.axis_size(axis)
    return lax.ppermute(value, axis, [(i, (i + shift * stride) % size) for i in range(size)])


def chip_shift(value, k, back):
    size = lax.axis_size("group")
    chips = size // 2
    if chips & (chips - 1):
        return rotate(value, "group", -k if back else k, 2)
    return lax.ppermute(value, "group", [(i, i ^ (2 * k)) for i in range(size)])


def other_core(value):
    return lax.ppermute(value, "group", [(i, i ^ 1) for i in range(lax.axis_size("group"))])


def pack(tokens, routes, gate_weights):
    zero = jnp.zeros((), jnp.bfloat16)
    width = tokens.shape[1]
    column = lax.broadcasted_iota(jnp.int32, (tokens.shape[0], width + LANES), 1)
    inside = jnp.where(column < width, 0, 1)
    packed = lax.pad(tokens, zero, ((0, 0, 0), (0, LANES, 0)))
    first = width
    for side in (routes, gate_weights):
        last = first + side.shape[1]
        side = lax.pad(side, jnp.zeros((), side.dtype), ((0, 0, 0), (first, width + LANES - last, 0)))
        if side.dtype == jnp.int32:
            side = (side * inside).astype(jnp.bfloat16)
        packed = packed + side
        first = last
    return packed


def fetch_kernel(source_ref, after_ref, out_ref, sem):
    copy = pltpu.make_async_copy(source_ref.at[:, : out_ref.shape[1]], out_ref, sem)
    copy.start()
    copy.wait()


def fetch(weights, depth, after, limit):
    shape = (weights.shape[0], depth, weights.shape[2])
    nbytes = shape[0] * shape[1] * shape[2] * 2
    return pl.pallas_call(
        fetch_kernel,
        out_shape=jax.ShapeDtypeStruct(shape, weights.dtype),
        in_specs=[pl.BlockSpec(memory_space=pl.ANY)] * 2,
        out_specs=pl.BlockSpec(memory_space=pltpu.VMEM),
        scratch_shapes=[pltpu.SemaphoreType.DMA],
        compiler_params=pltpu.CompilerParams(vmem_limit_bytes=limit << 20),
        cost_estimate=pl.CostEstimate(flops=0, bytes_accessed=nbytes, transcendentals=0),
    )(weights, after)


def experts_kernel(count, *refs):
    pieces, (gate_ref, up_ref, gate_hbm, down_hbm), outs = refs[:count], refs[count : count + 4], refs[count + 4 : -6]
    down_ref, rest_ref, x_ref, acts_ref, sems, rest_sem = refs[-6:]
    depth, width = down_ref.shape
    pairs = gate_ref.shape[0]
    hidden_here = depth // pairs
    block = outs[0].shape[0]
    chunks = sems.shape[0]
    step = width // chunks

    def piece(c):
        columns = pl.ds(pl.multiple_of(c * step, LANES), step)
        return columns, pltpu.make_async_copy(down_hbm.at[:, columns], down_ref.at[:, columns], sems.at[c])

    early = gate_ref.shape[1]
    rest = pltpu.make_async_copy(gate_hbm.at[:, early:], rest_ref, rest_sem)
    rest.start()
    for c in range(chunks):
        piece(c)[1].start()
    group = lax.axis_index("group").astype(jnp.float32)
    first = 0
    while first < x_ref.shape[0]:
        for part in pieces:
            x_ref[first : first + part.shape[0], :] = part[:, :width]
            first += part.shape[0]
    side = jnp.concatenate([part[:, width:] for part in pieces], axis=0).astype(jnp.float32)
    rows = side.shape[0]
    acts_ref[...] = jnp.zeros_like(acts_ref)

    half = early // 2

    def enter(c, carry):
        depths = pl.ds(pl.multiple_of(c * half, LANES), half)
        x = x_ref[:, depths]
        for e in range(pairs):
            acts_ref[e, 0] += jnp.dot(x, gate_ref[e, depths, :], preferred_element_type=jnp.float32)
            acts_ref[e, 1] += jnp.dot(x, up_ref[e, depths, :], preferred_element_type=jnp.float32)
        return carry

    lax.fori_loop(0, 2, enter, 0)
    rest.wait()
    x = x_ref[:, early:]
    for e in range(pairs):
        acts_ref[e, 0] += jnp.dot(x, rest_ref[e], preferred_element_type=jnp.float32)
        acts_ref[e, 1] += jnp.dot(x, up_ref[e, early:], preferred_element_type=jnp.float32)
    hidden, weight = [], []
    for e in range(pairs):
        total = jnp.zeros((rows, 1), jnp.float32)
        for k in range(GROUPS_ROW):
            column = GROUPS_ROW + k * pairs + e
            total = total + jnp.where(side[:, k : k + 1] == group, side[:, column : column + 1], 0.0)
        weight.append(total)
        gate_act = acts_ref[e, 0]
        hidden.append((gate_act / (1.0 + jnp.exp(-gate_act)) * acts_ref[e, 1]).astype(jnp.bfloat16))

    def down(c, carry):
        columns, copy = piece(c)
        copy.wait()
        y = jnp.zeros((rows, step), jnp.float32)
        for e in range(pairs):
            part = down_ref[e * hidden_here : (e + 1) * hidden_here, columns]
            y = y + weight[e] * jnp.dot(hidden[e], part, preferred_element_type=jnp.float32)[:rows]
        for i, out in enumerate(outs):
            out[:, columns] = y[i * block : (i + 1) * block].astype(out.dtype)
        return carry

    lax.fori_loop(0, chunks, down, 0)


def join_kernel(blocks, *refs):
    total = refs[0][...]
    for ref in refs[1:-blocks]:
        total = total + ref[...].astype(jnp.float32)
    height = total.shape[0] // blocks
    for i, out in enumerate(refs[-blocks:]):
        out[...] = total[i * height : (i + 1) * height].astype(out.dtype)


def join(values, blocks, first):
    shape = (values[0].shape[0] // blocks, values[0].shape[1])
    return pl.pallas_call(
        functools.partial(join_kernel, blocks),
        out_shape=[
            jax.ShapeDtypeStruct(shape, jnp.bfloat16 if first + i else jnp.float32) for i in range(blocks)
        ],
        compiler_params=pltpu.CompilerParams(vmem_limit_bytes=4 << 20),
    )(*values)


def on_device(tokens, routes, gate_weights, w_gate, w_up, w_down):
    chips = lax.axis_size("group") // 2
    locals_ = lax.axis_size("local")
    rows_here, width = tokens.shape
    pairs, _, hidden_here = w_gate.shape
    mine = pack(tokens, routes, gate_weights)
    early = width - width // 7
    others = [chip_shift(mine, k, False) for k in range(1, chips)]
    gate_here, others = lax.optimization_barrier((fetch(w_gate, early, mine, 38), others))
    line = jnp.concatenate([mine] + others, axis=0)
    crossed = [rotate(line, "local", k, 1) for k in range(1, locals_)]
    across_line = other_core(line)
    up_here, crossed = lax.optimization_barrier((fetch(w_up, width, line, 29), crossed))
    pieces = [line] + crossed + [across_line] + [other_core(part) for part in crossed]
    block = chips * rows_here
    rows = 2 * locals_ * block
    padded = rows * max(1, LEAST_ROWS // rows)
    outs = pl.pallas_call(
        functools.partial(experts_kernel, len(pieces)),
        out_shape=[jax.ShapeDtypeStruct((block, width), jnp.float32)] * locals_
        + [jax.ShapeDtypeStruct((block, width), jnp.bfloat16)] * locals_,
        in_specs=[pl.BlockSpec(memory_space=pltpu.VMEM)] * (len(pieces) + 2) + [pl.BlockSpec(memory_space=pl.ANY)] * 2,
        scratch_shapes=[
            pltpu.VMEM((pairs * hidden_here, width), jnp.bfloat16),
            pltpu.VMEM((pairs, width - early, hidden_here), jnp.bfloat16),
            pltpu.VMEM((padded, width), jnp.bfloat16),
            pltpu.VMEM((pairs, 2, padded, hidden_here), jnp.float32),
            pltpu.SemaphoreType.DMA((2 if padded <= LEAST_ROWS else 7,)),
            pltpu.SemaphoreType.DMA,
        ],
        compiler_params=pltpu.CompilerParams(vmem_limit_bytes=21 << 20),
    )(*pieces, gate_here, up_here, w_gate, w_down.reshape(pairs * hidden_here, width))
    totals = [None] * locals_
    for k in reversed(range(locals_)):
        totals[k] = outs[k] + other_core(outs[locals_ + k]).astype(jnp.float32)
    home = [None] * chips
    done = None
    for low, high in ((chips // 2, chips), (0, chips // 2)):
        if low == high:
            continue
        part = slice(low * rows_here, high * rows_here)
        sent = [totals[k][part].astype(jnp.bfloat16) for k in range(1, locals_)]
        if done is not None:
            sent, done = lax.optimization_barrier((sent, done))
        backs = [rotate(sent[k - 1], "local", -k, 1) for k in range(1, locals_)]
        home[low:high] = join([totals[0][part]] + backs, high - low, low)
        done = home[high - 1]
    result = home[0]
    for c in range(1, chips):
        result = result + chip_shift(home[c], c, True).astype(jnp.float32)
    return result.astype(jnp.bfloat16)


def solution(mesh):
    return jax.shard_map(
        on_device,
        mesh=mesh,
        in_specs=(
            P(("parts", "group", "local"), None),
            P(("parts", "group", "local"), None),
            P(("parts", "group", "local"), None),
            P("group", None, "local"),
            P("group", None, "local"),
            P("group", "local", None),
        ),
        out_specs=P(("parts", "group", "local"), None),
        check_vma=False,
    )
```

```python
import functools

import jax
import jax.numpy as jnp
from jax import lax
from jax.experimental import pallas as pl
from jax.experimental.pallas import tpu as pltpu
from jax.sharding import PartitionSpec as P

LANES = 128
LEAST_ROWS = 128
GROUPS_ROW = 4


def rotate(value, axis, shift, stride):
    size = lax.axis_size(axis)
    return lax.ppermute(value, axis, [(i, (i + shift * stride) % size) for i in range(size)])


def chip_shift(value, k, back):
    size = lax.axis_size("group")
    chips = size // 2
    if chips & (chips - 1):
        return rotate(value, "group", -k if back else k, 2)
    return lax.ppermute(value, "group", [(i, i ^ (2 * k)) for i in range(size)])


def other_core(value):
    return lax.ppermute(value, "group", [(i, i ^ 1) for i in range(lax.axis_size("group"))])


def pack(tokens, routes, gate_weights):
    zero = jnp.zeros((), jnp.bfloat16)
    width = tokens.shape[1]
    column = lax.broadcasted_iota(jnp.int32, (tokens.shape[0], width + LANES), 1)
    inside = jnp.where(column < width, 0, 1)
    packed = lax.pad(tokens, zero, ((0, 0, 0), (0, LANES, 0)))
    first = width
    for side in (routes, gate_weights):
        last = first + side.shape[1]
        side = lax.pad(side, jnp.zeros((), side.dtype), ((0, 0, 0), (first, width + LANES - last, 0)))
        if side.dtype == jnp.int32:
            side = (side * inside).astype(jnp.bfloat16)
        packed = packed + side
        first = last
    return packed


def fetch_kernel(source_ref, after_ref, out_ref, sem):
    copy = pltpu.make_async_copy(source_ref.at[:, : out_ref.shape[1]], out_ref, sem)
    copy.start()
    copy.wait()


def fetch(weights, depth, after, limit):
    shape = (weights.shape[0], depth, weights.shape[2])
    nbytes = shape[0] * shape[1] * shape[2] * 2
    return pl.pallas_call(
        fetch_kernel,
        out_shape=jax.ShapeDtypeStruct(shape, weights.dtype),
        in_specs=[pl.BlockSpec(memory_space=pl.ANY)] * 2,
        out_specs=pl.BlockSpec(memory_space=pltpu.VMEM),
        scratch_shapes=[pltpu.SemaphoreType.DMA],
        compiler_params=pltpu.CompilerParams(vmem_limit_bytes=limit << 20),
        cost_estimate=pl.CostEstimate(flops=0, bytes_accessed=nbytes, transcendentals=0),
    )(weights, after)


def experts_kernel(count, *refs):
    pieces, (gate_ref, up_ref, gate_hbm, down_hbm), outs = refs[:count], refs[count : count + 4], refs[count + 4 : -6]
    down_ref, rest_ref, x_ref, acts_ref, sems, rest_sem = refs[-6:]
    depth, width = down_ref.shape
    pairs = gate_ref.shape[0]
    hidden_here = depth // pairs
    block = outs[0].shape[0]
    chunks = sems.shape[0]
    step = width // chunks

    def piece(c):
        columns = pl.ds(pl.multiple_of(c * step, LANES), step)
        return columns, pltpu.make_async_copy(down_hbm.at[:, columns], down_ref.at[:, columns], sems.at[c])

    early = gate_ref.shape[1]
    rest = pltpu.make_async_copy(gate_hbm.at[:, early:], rest_ref, rest_sem)
    rest.start()
    for c in range(chunks):
        piece(c)[1].start()
    group = lax.axis_index("group").astype(jnp.float32)
    first = 0
    while first < x_ref.shape[0]:
        for part in pieces:
            x_ref[first : first + part.shape[0], :] = part[:, :width]
            first += part.shape[0]
    side = jnp.concatenate([part[:, width:] for part in pieces], axis=0).astype(jnp.float32)
    rows = side.shape[0]
    acts_ref[...] = jnp.zeros_like(acts_ref)

    half = early // 2

    def enter(c, carry):
        depths = pl.ds(pl.multiple_of(c * half, LANES), half)
        x = x_ref[:, depths]
        for e in range(pairs):
            acts_ref[e, 0] += jnp.dot(x, gate_ref[e, depths, :], preferred_element_type=jnp.float32)
            acts_ref[e, 1] += jnp.dot(x, up_ref[e, depths, :], preferred_element_type=jnp.float32)
        return carry

    lax.fori_loop(0, 2, enter, 0)
    rest.wait()
    x = x_ref[:, early:]
    hidden, weight = [], []
    for e in range(pairs):
        total = jnp.zeros((rows, 1), jnp.float32)
        for k in range(GROUPS_ROW):
            column = GROUPS_ROW + k * pairs + e
            total = total + jnp.where(side[:, k : k + 1] == group, side[:, column : column + 1], 0.0)
        weight.append(total)
        gate_act = acts_ref[e, 0] + jnp.dot(x, rest_ref[e], preferred_element_type=jnp.float32)
        up_act = acts_ref[e, 1] + jnp.dot(x, up_ref[e, early:], preferred_element_type=jnp.float32)
        hidden.append((gate_act / (1.0 + jnp.exp(-gate_act)) * up_act).astype(jnp.bfloat16))

    def down(c, carry):
        columns, copy = piece(c)
        copy.wait()
        y = jnp.zeros((rows, step), jnp.float32)
        for e in range(pairs):
            part = down_ref[e * hidden_here : (e + 1) * hidden_here, columns]
            y = y + weight[e] * jnp.dot(hidden[e], part, preferred_element_type=jnp.float32)[:rows]
        for i, out in enumerate(outs):
            out[:, columns] = y[i * block : (i + 1) * block].astype(out.dtype)
        return carry

    lax.fori_loop(0, chunks, down, 0)


def join_kernel(blocks, *refs):
    total = refs[0][...]
    for ref in refs[1:-blocks]:
        total = total + ref[...].astype(jnp.float32)
    height = total.shape[0] // blocks
    for i, out in enumerate(refs[-blocks:]):
        out[...] = total[i * height : (i + 1) * height].astype(out.dtype)


def join(values, blocks, first):
    shape = (values[0].shape[0] // blocks, values[0].shape[1])
    return pl.pallas_call(
        functools.partial(join_kernel, blocks),
        out_shape=[
            jax.ShapeDtypeStruct(shape, jnp.bfloat16 if first + i else jnp.float32) for i in range(blocks)
        ],
        compiler_params=pltpu.CompilerParams(vmem_limit_bytes=4 << 20),
    )(*values)


def on_device(tokens, routes, gate_weights, w_gate, w_up, w_down):
    chips = lax.axis_size("group") // 2
    locals_ = lax.axis_size("local")
    rows_here, width = tokens.shape
    pairs, _, hidden_here = w_gate.shape
    mine = pack(tokens, routes, gate_weights)
    early = width - width // 7
    others = [chip_shift(mine, k, False) for k in range(1, chips)]
    gate_here, others = lax.optimization_barrier((fetch(w_gate, early, mine, 38), others))
    line = jnp.concatenate([mine] + others, axis=0)
    crossed = [rotate(line, "local", k, 1) for k in range(1, locals_)]
    across_line = other_core(line)
    up_here, crossed = lax.optimization_barrier((fetch(w_up, width, line, 29), crossed))
    pieces = [line] + crossed + [across_line] + [other_core(part) for part in crossed]
    block = chips * rows_here
    rows = 2 * locals_ * block
    padded = rows * max(1, LEAST_ROWS // rows)
    outs = pl.pallas_call(
        functools.partial(experts_kernel, len(pieces)),
        out_shape=[jax.ShapeDtypeStruct((block, width), jnp.float32)] * locals_
        + [jax.ShapeDtypeStruct((block, width), jnp.bfloat16)] * locals_,
        in_specs=[pl.BlockSpec(memory_space=pltpu.VMEM)] * (len(pieces) + 2) + [pl.BlockSpec(memory_space=pl.ANY)] * 2,
        scratch_shapes=[
            pltpu.VMEM((pairs * hidden_here, width), jnp.bfloat16),
            pltpu.VMEM((pairs, width - early, hidden_here), jnp.bfloat16),
            pltpu.VMEM((padded, width), jnp.bfloat16),
            pltpu.VMEM((pairs, 2, padded, hidden_here), jnp.float32),
            pltpu.SemaphoreType.DMA((2 if padded <= LEAST_ROWS else 7,)),
            pltpu.SemaphoreType.DMA,
        ],
        compiler_params=pltpu.CompilerParams(vmem_limit_bytes=21 << 20),
    )(*pieces, gate_here, up_here, w_gate, w_down.reshape(pairs * hidden_here, width))
    totals = [None] * locals_
    for k in reversed(range(locals_)):
        away = outs[locals_ + k]
        if k + 1 < locals_:
            away, _ = lax.optimization_barrier((away, totals[k + 1]))
        totals[k] = outs[k] + other_core(away).astype(jnp.float32)
    base = [total[:rows_here] for total in totals]
    if chips > 1:
        near = [total[rows_here : 2 * rows_here].astype(jnp.bfloat16) for total in totals]
        near = chip_shift(jnp.concatenate(near, axis=0), 1, True).astype(jnp.float32)
        base = [value + near[k * rows_here : (k + 1) * rows_here] for k, value in enumerate(base)]
    home = []
    if chips > 2:
        far = [total[2 * rows_here :] for total in totals]
        backs = [rotate(far[k].astype(jnp.bfloat16), "local", -k, 1) for k in range(1, locals_)]
        home = join([far[0]] + backs, chips - 2, 2)
    result = base[0]
    for k in range(1, locals_):
        sent = base[k].astype(jnp.bfloat16)
        result = result + rotate(sent, "local", -k, 1).astype(jnp.float32)
    for c, value in enumerate(home):
        result = result + chip_shift(value, c + 2, True).astype(jnp.float32)
    return result.astype(jnp.bfloat16)


def solution(mesh):
    return jax.shard_map(
        on_device,
        mesh=mesh,
        in_specs=(
            P(("parts", "group", "local"), None),
            P(("parts", "group", "local"), None),
            P(("parts", "group", "local"), None),
            P("group", None, "local"),
            P("group", None, "local"),
            P("group", "local", None),
        ),
        out_specs=P(("parts", "group", "local"), None),
        check_vma=False,
    )
```
